128 devices in a mesh: section: 8 (over y, z_hi), tensor: 16 (over x, z_lo, core).
Axes of the slice: x: 4, y: 4, z: 4 (z_hi: 2, z_lo: 2; z = z_hi * 2 + z_lo), core: 2. Of those that a mesh axis runs over, the one named last changes fastest.
Arguments:
- top_grad: bfloat16 [1, 2048, 2304], P(None, 'tensor'), may hold values from -6 to 6
- down_weight: bfloat16 [8, 18432, 2304], P('section', 'tensor'), may hold values from -0.046875 to 0.046875
- up_weight: bfloat16 [8, 2304, 18432], P('section', None, 'tensor'), may hold values from -0.125 to 0.125
- gate_pre: bfloat16 [8, 1, 2048, 18432], P('section', None, None, 'tensor'), may hold values from -6 to 6
Outputs:
- input_grad: bfloat16 [8, 1, 2048, 2304], P('section', None, 'tensor')
The draws below stay inside these ranges and needn't reach their ends.
All inputs are finite; a program needn't handle non-finite values.
Results may differ from the reference program's by a relative error of at most 0.04.
Values may be sent and summed in bfloat16 or wider, within the bound.
A program may use at most 128 MiB of HBM per device.

```python
import jax
import jax.numpy as jnp
from jax import lax

D = 2304
FF = 18432
MICRO = 1
SECTIONS = 8
TOKENS = 2048
N_TENSOR = 16


def steps_of(own_key, shape, split, least, high):
    level = 1.0
    for position, parts in split:
        draws = jax.random.uniform(jax.random.fold_in(jax.random.fold_in(own_key, 6), position), (parts,), jnp.float32, least / len(split), high / len(split))
        level = level * jnp.repeat(jnp.exp(draws), shape[position] // parts).reshape((-1,) + (1,) * (len(shape) - 1 - position))
    return level


def normal_values(key, extent, width, limit, pieces=(), held_as=jnp.bfloat16):
    level = steps_of(key, extent, pieces, -0.22, 0.18) if pieces else 1.0
    array = jax.random.normal(key, extent, jnp.float32) * width * level
    return jnp.minimum(jnp.maximum(array, -limit), limit).astype(held_as)


def setup_inputs(seed: int = 0) -> dict:
    arg_keys = jax.random.split(jax.random.key(seed), 5)
    top_grad = normal_values(arg_keys[0], (MICRO, TOKENS, D), 1.0, 6.0, ((1, 16),))
    down_weight = normal_values(arg_keys[1], (SECTIONS, FF, D), FF ** -0.5, 0.046875, ((0, 8), (1, 16)))
    up_weight = normal_values(arg_keys[2], (SECTIONS, D, FF), D ** -0.5, 0.125, ((0, 8), (2, 16)))
    gate_pre = normal_values(arg_keys[3], (SECTIONS, MICRO, TOKENS, FF), 1.0, 6.0, ((0, 8), (3, 16)))
    return dict(top_grad=top_grad, down_weight=down_weight, up_weight=up_weight, gate_pre=gate_pre)


def section_unit(grad_out, down_proj, up_proj, gate_saved):
    grad_hidden = jnp.dot(grad_out, down_proj.T, preferred_element_type=jnp.float32)
    gate_value = jax.nn.gelu(gate_saved.astype(jnp.float32), approximate=True)
    grad_up = (grad_hidden * gate_value).astype(jnp.bfloat16)
    block_cols = up_proj.shape[1] // N_TENSOR

    def add_block(total, block_index):
        first_col = block_index * block_cols
        left_cols = lax.dynamic_slice_in_dim(grad_up, first_col, block_cols, 1)
        right_cols = lax.dynamic_slice_in_dim(up_proj, first_col, block_cols, 1)
        term = jnp.dot(left_cols, right_cols.T, preferred_element_type=jnp.float32)
        rounded = lax.optimization_barrier(term.astype(jnp.bfloat16))
        return total + rounded.astype(jnp.float32), None

    initial = jnp.zeros(grad_out.shape, jnp.float32)
    total, _ = lax.scan(add_block, initial, jnp.arange(N_TENSOR, dtype=jnp.int32))
    return (grad_out.astype(jnp.float32) + total).astype(jnp.bfloat16)


def reference(top_grad, down_weight, up_weight, gate_pre):
    current = [top_grad[micro_index] for micro_index in range(MICRO)]
    section_results = [None] * SECTIONS
    for section_index in reversed(range(SECTIONS)):
        produced = []
        for micro_index in range(MICRO):
            produced.append(section_unit(current[micro_index], down_weight[section_index], up_weight[section_index], gate_pre[section_index, micro_index]))
        section_results[section_index] = jnp.stack(produced)
        current = produced
    return jnp.stack(section_results)
```

```python
import functools

import jax
import jax.numpy as jnp
from jax import lax
from jax.experimental import pallas as pl
from jax.experimental.pallas import tpu as pltpu
from jax.sharding import PartitionSpec as P

MESH = pl.DeviceIdType.MESH
BLOCK = 16
F32 = jnp.float32
BF16 = jnp.bfloat16
NN = (((1,), (0,)), ((), ()))


def gelu(v):
    return 0.5 * v * (1.0 + jnp.tanh(0.7978845608028654 * (v + 0.044715 * (v * v * v))))


def kernel(
    sections, chips, chunks,
    top_hbm, down_hbm, up_hbm, gate_hbm, out_hbm,
    top, down, up, gate, feed, held, act, hidden, grad_up, own_part, sib_part, sib_recv, pair, terms, result, out,
    load_sem, feed_send, feed_recv, own_sem, in_send, in_recv, swap_send, swap_recv, part_send, part_recv,
    term_send, term_recv, out_send, out_recv, store_sem,
):
    section = lax.axis_index("section")
    tensor = lax.axis_index("tensor")
    chip = lax.div(tensor, 2)
    core = lax.rem(tensor, 2)
    other = 1 - core
    sibling = chip * 2 + other
    half = held.shape[-1]
    per_core = chunks // 2
    last = sections - 1

    def wait_for(ref, sem):
        pltpu.make_async_copy(ref, ref, sem).wait()

    def remote(src, dst, send, recv, to_section, to_tensor):
        return pltpu.make_async_remote_copy(
            src_ref=src, dst_ref=dst, send_sem=send, recv_sem=recv,
            device_id={"section": to_section, "tensor": to_tensor}, device_id_type=MESH,
        )

    def rows_of(index):
        return pl.ds(pl.multiple_of(index * BLOCK, BLOCK), BLOCK)

    def cols_of(index):
        return pl.ds(pl.multiple_of(index * half, 128), half)

    loads = [
        pltpu.make_async_copy(top_hbm, top, load_sem.at[0]),
        pltpu.make_async_copy(gate_hbm, gate, load_sem.at[1]),
        pltpu.make_async_copy(down_hbm, down, load_sem.at[2]),
        pltpu.make_async_copy(up_hbm, up, load_sem.at[3]),
    ]
    for load in loads:
        load.start()

    barrier = pltpu.get_barrier_semaphore()

    def greet(to_section, to_tensor):
        pl.semaphore_signal(
            barrier, inc=1, device_id={"section": to_section, "tensor": to_tensor}, device_id_type=MESH
        )

    greet(section, sibling)
    for step in range(1, chips):
        greet(section, lax.rem(chip + step, chips) * 2 + core)

    @pl.when(section > 0)
    def _():
        for step in range(chips):
            greet(section - 1, lax.rem(chip + step, chips) * 2 + core)

    @pl.when(section < last)
    def _():
        for step in range(chips):
            greet(section + 1, lax.rem(chip + step, chips) * 2 + core)

    pl.semaphore_wait(
        barrier, chips + jnp.where(section > 0, chips, 0) + jnp.where(section < last, chips, 0)
    )

    loads[0].wait()

    def send_feed(c):
        block = feed.at[pl.ds(pl.multiple_of(c * BLOCK, BLOCK), BLOCK)]
        for step in range(1, chips):
            remote(
                block, held.at[c, core, rows_of(chip)], in_send.at[c], in_recv.at[c],
                section, lax.rem(chip + step, chips) * 2 + core,
            ).start()
        pltpu.make_async_copy(block, held.at[c, core, rows_of(chip)], in_recv.at[c]).start()

    rows_here = per_core * BLOCK

    @pl.when(section == last)
    def _():
        mine = feed.at[pl.ds(pl.multiple_of(core * rows_here, BLOCK), rows_here)]
        swap = remote(top.at[:, cols_of(other)], mine, feed_send, feed_recv, section, sibling)
        swap.start()
        keep = pltpu.make_async_copy(top.at[:, cols_of(core)], mine, own_sem)
        keep.start()
        keep.wait()
        swap.wait()
        send_feed(0)
        if chunks > 1:
            send_feed(1)

    loads[1].wait()

    def finish(c):
        wait_for(terms.at[c, pl.ds(0, chips - 1)], term_recv.at[c])
        total = held[c, core, rows_of(chip), :].astype(F32)
        for j in range(chips):
            total = total + terms[c, j].astype(F32)
        result[c] = total.astype(BF16)

        @pl.when(section > 0)
        def _():
            for step in range(chips):
                remote(
                    result.at[c], held.at[c, core, rows_of(chip)], in_send.at[c], in_recv.at[c],
                    section - 1, lax.rem(chip + step, chips) * 2 + core,
                ).start()

        place = lax.rem(c, per_core)

        @pl.when(lax.div(c, per_core) == core)
        def _():
            out[core, rows_of(place), :] = result[c]

        @pl.when(lax.div(c, per_core) == other)
        def _():
            remote(
                result.at[c], out.at[core, rows_of(place)], out_send, out_recv, section, sibling
            ).start()

    def chunk_step(c, carry):
        act[...] = gelu(gate[:, c].reshape(chips * BLOCK, -1).astype(F32))

        wait_for(held.at[c, core], in_recv.at[c])
        remote(
            held.at[c, core], held.at[c, core], swap_send.at[c], swap_recv.at[c], section, sibling
        ).start()

        @pl.when(c == 0)
        def _():
            loads[2].wait()

        hidden[...] = lax.dot_general(held[c, core], down[core], NN, preferred_element_type=F32)
        wait_for(held.at[c, other], swap_recv.at[c])
        total = hidden[...] + lax.dot_general(
            held[c, other], down[other], NN, preferred_element_type=F32
        )
        grad_up[...] = (total * act[...]).astype(BF16)

        @pl.when(c == 0)
        def _():
            loads[3].wait()

        sib_part[c] = lax.dot_general(
            grad_up[...], up[other], NN, preferred_element_type=F32
        ).astype(BF16)
        remote(
            sib_part.at[c], sib_recv.at[c], part_send.at[c], part_recv.at[c], section, sibling
        ).start()
        own_part[...] = lax.dot_general(grad_up[...], up[core], NN, preferred_element_type=F32)

        @pl.when(c > 0)
        def _():
            finish(c - 1)

        wait_for(sib_recv.at[c], part_recv.at[c])
        pair[c] = (own_part[...] + sib_recv[c].astype(F32)).astype(BF16)
        for step in range(1, chips):
            to_chip = lax.rem(chip + step, chips)
            remote(
                pair.at[c, rows_of(to_chip)], terms.at[c, chip], term_send.at[c], term_recv.at[c],
                section, to_chip * 2 + core,
            ).start()
        terms[c, chip] = pair[c, rows_of(chip), :]

        @pl.when((section == last) & (c + 2 < chunks))
        def _():
            send_feed(c + 2)

        return carry

    lax.fori_loop(0, chunks, chunk_step, 0)
    finish(chunks - 1)

    wait_for(out.at[other], out_recv)
    stores = [
        pltpu.make_async_copy(out.at[h], out_hbm.at[:, pl.ds(h * half, half)], store_sem.at[h])
        for h in range(2)
    ]
    for store in stores:
        store.start()

    def drain(c, carry):
        wait_for(held.at[c, core], swap_send.at[c])
        wait_for(sib_part.at[c], part_send.at[c])
        wait_for(terms.at[c, pl.ds(0, chips - 1)], term_send.at[c])

        @pl.when(section > 0)
        def _():
            wait_for(terms.at[c], in_send.at[c])

        @pl.when(section == last)
        def _():
            wait_for(terms.at[c, pl.ds(0, chips - 1)], in_send.at[c])

        return carry

    lax.fori_loop(0, chunks, drain, 0)
    wait_for(out.at[core], out_send)
    for store in stores:
        store.wait()


def on_device(sections, top_grad, down_weight, up_weight, gate_pre):
    row_count, features = top_grad.shape[-2:]
    units = gate_pre.shape[-1]
    tokens = gate_pre.shape[2]
    devices = lax.axis_size("tensor")
    chips = devices // 2
    chunks = 2 * row_count // BLOCK
    half = features // 2
    rows = chips * BLOCK
    down = down_weight[0].T.reshape(2, half, units)
    up = up_weight[0].reshape(2, half, units).transpose(0, 2, 1)
    gate = gate_pre.reshape(chips, chunks, BLOCK, units)
    dma = pltpu.SemaphoreType.DMA
    produced = pl.pallas_call(
        functools.partial(kernel, sections, chips, chunks),
        name="chain",
        out_shape=jax.ShapeDtypeStruct((row_count, features), BF16),
        in_specs=[pl.BlockSpec(memory_space=pl.ANY)] * 4,
        out_specs=pl.BlockSpec(memory_space=pl.ANY),
        scratch_shapes=[
            pltpu.VMEM((row_count, features), BF16),
            pltpu.VMEM((2, half, units), BF16),
            pltpu.VMEM((2, units, half), BF16),
            pltpu.VMEM((chips, chunks, BLOCK, units), BF16),
            pltpu.VMEM((2 * row_count, half), BF16),
            pltpu.VMEM((chunks, 2, rows, half), BF16),
            pltpu.VMEM((rows, units), F32),
            pltpu.VMEM((rows, units), F32),
            pltpu.VMEM((rows, units), BF16),
            pltpu.VMEM((rows, half), F32),
            pltpu.VMEM((chunks, rows, half), BF16),
            pltpu.VMEM((chunks, rows, half), BF16),
            pltpu.VMEM((chunks, rows, half), BF16),
            pltpu.VMEM((chunks, chips, BLOCK, half), BF16),
            pltpu.VMEM((chunks, BLOCK, half), BF16),
            pltpu.VMEM((2, row_count, half), BF16),
            dma((4,)),
            dma,
            dma,
            dma,
            dma((chunks,)),
            dma((chunks,)),
            dma((chunks,)),
            dma((chunks,)),
            dma((chunks,)),
            dma((chunks,)),
            dma((chunks,)),
            dma((chunks,)),
            dma,
            dma,
            dma((2,)),
        ],
        compiler_params=pltpu.CompilerParams(
            collective_id=0, has_side_effects=True, vmem_limit_bytes=60 * 1024 * 1024
        ),
    )(top_grad[0], down, up, gate)
    return produced[None, None]


def solution(mesh):
    placed = (
        P(None, "tensor", None),
        P("section", "tensor", None),
        P("section", None, "tensor"),
        P("section", None, None, "tensor"),
    )
    return jax.shard_map(
        functools.partial(on_device, mesh.shape["section"]),
        mesh=mesh,
        in_specs=placed,
        out_specs=P("section", None, "tensor", None),
        check_vma=False,
    )
```

```python
import functools

import jax
import jax.numpy as jnp
from jax import lax
from jax.experimental import pallas as pl
from jax.experimental.pallas import tpu as pltpu
from jax.sharding import PartitionSpec as P

MESH = pl.DeviceIdType.MESH
BLOCK = 16
AHEAD = 3
F32 = jnp.float32
BF16 = jnp.bfloat16
NN = (((1,), (0,)), ((), ()))


def gelu(v):
    return 0.5 * v * (1.0 + jnp.tanh(0.7978845608028654 * (v + 0.044715 * (v * v * v))))


def kernel(
    sections, chips, chunks,
    top_hbm, down_hbm, up_hbm, gate_hbm, out_hbm,
    top, down_raw, up_raw, down, up, gate, feed, held, act, hidden, grad_up, own_part, sib_part, sib_recv, pair, terms, result, out,
    load_sem, feed_send, feed_recv, own_sem, hop_send, hop_recv, in_send, in_recv, swap_send, swap_recv, part_send, part_recv,
    term_send, term_recv, out_send, out_recv, store_sem,
):
    section = lax.axis_index("section")
    tensor = lax.axis_index("tensor")
    chip = lax.div(tensor, 2)
    core = lax.rem(tensor, 2)
    other = 1 - core
    sibling = chip * 2 + other
    half = held.shape[-1]
    per_core = chunks // 2
    last = sections - 1

    def wait_for(ref, sem):
        pltpu.make_async_copy(ref, ref, sem).wait()

    def remote(src, dst, send, recv, to_section, to_tensor):
        return pltpu.make_async_remote_copy(
            src_ref=src, dst_ref=dst, send_sem=send, recv_sem=recv,
            device_id={"section": to_section, "tensor": to_tensor}, device_id_type=MESH,
        )

    def rows_of(index):
        return pl.ds(pl.multiple_of(index * BLOCK, BLOCK), BLOCK)

    def cols_of(index):
        return pl.ds(pl.multiple_of(index * half, 128), half)

    loads = [
        pltpu.make_async_copy(top_hbm, top, load_sem.at[0]),
        pltpu.make_async_copy(gate_hbm, gate, load_sem.at[1]),
        pltpu.make_async_copy(down_hbm, down_raw, load_sem.at[2]),
        pltpu.make_async_copy(up_hbm, up_raw, load_sem.at[3]),
    ]
    for load in loads:
        load.start()

    barrier = pltpu.get_barrier_semaphore()

    def greet(to_section, to_tensor):
        pl.semaphore_signal(
            barrier, inc=1, device_id={"section": to_section, "tensor": to_tensor}, device_id_type=MESH
        )

    greet(section, sibling)
    for step in range(1, chips):
        greet(section, lax.rem(chip + step, chips) * 2 + core)

    facing = chip + 1 - 2 * lax.rem(chip, 2)

    @pl.when(section > 0)
    def _():
        greet(section - 1, facing * 2 + core)

    @pl.when(section < last)
    def _():
        greet(section + 1, facing * 2 + core)

    pl.semaphore_wait(barrier, chips + jnp.where(section > 0, 1, 0) + jnp.where(section < last, 1, 0))

    loads[0].wait()

    def spread(block, c, index):
        for step in range(1, chips):
            remote(
                block, held.at[c, core, rows_of(index)], in_send.at[c], in_recv.at[c],
                section, lax.rem(chip + step, chips) * 2 + core,
            ).start()

    def send_feed(c):
        block = feed.at[pl.ds(pl.multiple_of(c * BLOCK, BLOCK), BLOCK)]
        spread(block, c, chip)
        pltpu.make_async_copy(block, held.at[c, core, rows_of(chip)], hop_recv.at[c]).start()

    def forward(c):
        block = held.at[c, core, rows_of(facing)]
        wait_for(block, hop_recv.at[c])
        spread(block, c, facing)

    rows_here = per_core * BLOCK

    @pl.when(section == last)
    def _():
        mine = feed.at[pl.ds(pl.multiple_of(core * rows_here, BLOCK), rows_here)]
        swap = remote(top.at[:, cols_of(other)], mine, feed_send, feed_recv, section, sibling)
        swap.start()
        keep = pltpu.make_async_copy(top.at[:, cols_of(core)], mine, own_sem)
        keep.start()
        keep.wait()
        swap.wait()
        for c in range(min(AHEAD, chunks)):
            send_feed(c)

    loads[1].wait()

    def finish(c):
        wait_for(terms.at[c, pl.ds(0, chips - 1)], term_recv.at[c])
        total = held[c, core, rows_of(chip), :].astype(F32)
        for j in range(chips):
            total = total + terms[c, j].astype(F32)
        result[c] = total.astype(BF16)

        @pl.when(section > 0)
        def _():
            remote(
                result.at[c], held.at[c, core, rows_of(chip)], hop_send.at[c], hop_recv.at[c],
                section - 1, facing * 2 + core,
            ).start()

        place = lax.rem(c, per_core)

        @pl.when(lax.div(c, per_core) == core)
        def _():
            out[core, rows_of(place), :] = result[c]

        @pl.when(lax.div(c, per_core) == other)
        def _():
            remote(
                result.at[c], out.at[core, rows_of(place)], out_send, out_recv, section, sibling
            ).start()

    def chunk_step(c, carry):
        act[...] = gelu(gate[:, c].reshape(chips * BLOCK, -1).astype(F32))

        @pl.when(section == last)
        def _():
            wait_for(held.at[c, core, rows_of(chip)], hop_recv.at[c])

        wait_for(terms.at[c, pl.ds(0, chips - 1)], in_recv.at[c])
        remote(
            held.at[c, core], held.at[c, core], swap_send.at[c], swap_recv.at[c], section, sibling
        ).start()

        hidden[...] = lax.dot_general(held[c, core], down[core], NN, preferred_element_type=F32)

        @pl.when((section < last) & (c + 1 < chunks))
        def _():
            forward(c + 1)

        wait_for(held.at[c, other], swap_recv.at[c])
        total = hidden[...] + lax.dot_general(
            held[c, other], down[other], NN, preferred_element_type=F32
        )
        grad_up[...] = (total * act[...]).astype(BF16)

        sib_part[c] = lax.dot_general(
            grad_up[...], up[other], NN, preferred_element_type=F32
        ).astype(BF16)
        remote(
            sib_part.at[c], sib_recv.at[c], part_send.at[c], part_recv.at[c], section, sibling
        ).start()
        own_part[...] = lax.dot_general(grad_up[...], up[core], NN, preferred_element_type=F32)

        wait_for(sib_recv.at[c], part_recv.at[c])
        pair[c] = (own_part[...] + sib_recv[c].astype(F32)).astype(BF16)
        for step in range(1, chips):
            to_chip = lax.rem(chip + step, chips)
            remote(
                pair.at[c, rows_of(to_chip)], terms.at[c, chip], term_send.at[c], term_recv.at[c],
                section, to_chip * 2 + core,
            ).start()
        terms[c, chip] = pair[c, rows_of(chip), :]

        @pl.when((section == last) & (c + AHEAD < chunks))
        def _():
            send_feed(c + AHEAD)

        @pl.when(c > 0)
        def _():
            finish(c - 1)

        return carry

    tiles = half // 128

    def turn_down(i, carry):
        for h in range(2):
            down[h, pl.ds(pl.multiple_of(i * 128, 128), 128), :] = down_raw[
                :, pl.ds(pl.multiple_of(h * half + i * 128, 128), 128)
            ].T
        return carry

    def turn_up(i, carry):
        for h in range(2):
            up[h, :, pl.ds(pl.multiple_of(i * 128, 128), 128)] = up_raw[
                pl.ds(pl.multiple_of(h * half + i * 128, 128), 128), :
            ].T
        return carry

    loads[2].wait()
    lax.fori_loop(0, tiles, turn_down, 0)
    loads[3].wait()
    lax.fori_loop(0, tiles, turn_up, 0)

    @pl.when(section < last)
    def _():
        forward(0)

    lax.fori_loop(0, chunks, chunk_step, 0)
    finish(chunks - 1)

    wait_for(out.at[other], out_recv)
    stores = [
        pltpu.make_async_copy(out.at[h], out_hbm.at[:, pl.ds(h * half, half)], store_sem.at[h])
        for h in range(2)
    ]
    for store in stores:
        store.start()

    def drain(c, carry):
        wait_for(held.at[c, core], swap_send.at[c])
        wait_for(sib_part.at[c], part_send.at[c])
        wait_for(terms.at[c, pl.ds(0, chips - 1)], term_send.at[c])

        wait_for(terms.at[c, pl.ds(0, chips - 1)], in_send.at[c])

        @pl.when(section > 0)
        def _():
            wait_for(result.at[c], hop_send.at[c])

        return carry

    lax.fori_loop(0, chunks, drain, 0)
    wait_for(out.at[core], out_send)
    for store in stores:
        store.wait()


def on_device(sections, top_grad, down_weight, up_weight, gate_pre):
    row_count, features = top_grad.shape[-2:]
    units = gate_pre.shape[-1]
    tokens = gate_pre.shape[2]
    devices = lax.axis_size("tensor")
    chips = devices // 2
    chunks = 2 * row_count // BLOCK
    half = features // 2
    rows = chips * BLOCK
    gate = gate_pre.reshape(chips, chunks, BLOCK, units)
    dma = pltpu.SemaphoreType.DMA
    produced = pl.pallas_call(
        functools.partial(kernel, sections, chips, chunks),
        name="chain",
        out_shape=jax.ShapeDtypeStruct((row_count, features), BF16),
        in_specs=[pl.BlockSpec(memory_space=pl.ANY)] * 4,
        out_specs=pl.BlockSpec(memory_space=pl.ANY),
        scratch_shapes=[
            pltpu.VMEM((row_count, features), BF16),
            pltpu.VMEM((units, features), BF16),
            pltpu.VMEM((features, units), BF16),
            pltpu.VMEM((2, half, units), BF16),
            pltpu.VMEM((2, units, half), BF16),
            pltpu.VMEM((chips, chunks, BLOCK, units), BF16),
            pltpu.VMEM((2 * row_count, half), BF16),
            pltpu.VMEM((chunks, 2, rows, half), BF16),
            pltpu.VMEM((rows, units), F32),
            pltpu.VMEM((rows, units), F32),
            pltpu.VMEM((rows, units), BF16),
            pltpu.VMEM((rows, half), F32),
            pltpu.VMEM((chunks, rows, half), BF16),
            pltpu.VMEM((chunks, rows, half), BF16),
            pltpu.VMEM((chunks, rows, half), BF16),
            pltpu.VMEM((chunks, chips, BLOCK, half), BF16),
            pltpu.VMEM((chunks, BLOCK, half), BF16),
            pltpu.VMEM((2, row_count, half), BF16),
            dma((4,)),
            dma,
            dma,
            dma,
            dma((chunks,)),
            dma((chunks,)),
            dma((chunks,)),
            dma((chunks,)),
            dma((chunks,)),
            dma((chunks,)),
            dma((chunks,)),
            dma((chunks,)),
            dma((chunks,)),
            dma((chunks,)),
            dma,
            dma,
            dma((2,)),
        ],
        compiler_params=pltpu.CompilerParams(
            collective_id=0, has_side_effects=True, vmem_limit_bytes=60 * 1024 * 1024
        ),
    )(top_grad[0], down_weight[0], up_weight[0], gate)
    return produced[None, None]


def solution(mesh):
    placed = (
        P(None, "tensor", None),
        P("section", "tensor", None),
        P("section", None, "tensor"),
        P("section", None, None, "tensor"),
    )
    return jax.shard_map(
        functools.partial(on_device, mesh.shape["section"]),
        mesh=mesh,
        in_specs=placed,
        out_specs=P("section", None, "tensor", None),
        check_vma=False,
    )
```

```python
import functools

import jax
import jax.numpy as jnp
from jax import lax
from jax.experimental import pallas as pl
from jax.experimental.pallas import tpu as pltpu
from jax.sharding import PartitionSpec as P

MESH = pl.DeviceIdType.MESH
BLOCK = 16
ORDER = ((2, 1), (2, 0), (1, 1), (3, 1), (1, 0), (3, 0), (0, 1))
AHEAD = 3
PARTS = ((0, 512), (512, 640))
F32 = jnp.float32
BF16 = jnp.bfloat16
NN = (((1,), (0,)), ((), ()))


def gelu(v):
    return 0.5 * v * (1.0 + jnp.tanh(0.7978845608028654 * (v + 0.044715 * (v * v * v))))


def kernel(
    sections, chips, chunks,
    top_hbm, down_hbm, up_hbm, gate_hbm, out_hbm,
    down_raw, up_raw, down, up, gate, feed, held, act, hidden, grad_up, own_part, sib_part, sib_recv, pair, terms, result, out,
    load_sem, feed_send, feed_recv, own_sem, hop_send, hop_recv, in_send, in_recv, swap_send, swap_recv, part_send, part_recv,
    term_send, term_recv, out_send, out_recv, store_sem,
):
    section = lax.axis_index("section")
    tensor = lax.axis_index("tensor")
    chip = lax.div(tensor, 2)
    core = lax.rem(tensor, 2)
    other = 1 - core
    sibling = chip * 2 + other
    half = held.shape[-1]
    per_core = chunks // 2
    last = sections - 1

    def wait_for(ref, sem):
        pltpu.make_async_copy(ref, ref, sem).wait()

    def remote(src, dst, send, recv, to_section, to_tensor):
        return pltpu.make_async_remote_copy(
            src_ref=src, dst_ref=dst, send_sem=send, recv_sem=recv,
            device_id={"section": to_section, "tensor": to_tensor}, device_id_type=MESH,
        )

    def peer(step, flip):
        return lax.rem(lax.div(chip, 2) + step, chips // 2) * 2 + lax.rem(chip + flip, 2)

    parts = [pl.ds(0, half)] if half < 1152 else [pl.ds(start, size) for start, size in PARTS]

    def rows_of(index):
        return pl.ds(pl.multiple_of(index * BLOCK, BLOCK), BLOCK)

    def cols_of(index):
        return pl.ds(pl.multiple_of(index * half, 128), half)

    loads = [
        pltpu.make_async_copy(gate_hbm, gate, load_sem.at[0]),
        pltpu.make_async_copy(down_hbm, down_raw, load_sem.at[1]),
        pltpu.make_async_copy(up_hbm, up_raw, load_sem.at[2]),
    ]
    for load in loads:
        load.start()

    barrier = pltpu.get_barrier_semaphore()

    def greet(to_section, to_tensor):
        pl.semaphore_signal(
            barrier, inc=1, device_id={"section": to_section, "tensor": to_tensor}, device_id_type=MESH
        )

    greet(section, sibling)
    for step in range(1, chips):
        greet(section, lax.rem(chip + step, chips) * 2 + core)

    facing = chip + 1 - 2 * lax.rem(chip, 2)

    @pl.when(section > 0)
    def _():
        greet(section - 1, facing * 2 + core)

    @pl.when(section < last)
    def _():
        greet(section + 1, facing * 2 + core)

    pl.semaphore_wait(barrier, chips + jnp.where(section > 0, 1, 0) + jnp.where(section < last, 1, 0))

    def spread(block, c, index, p):
        for relation in ORDER:
            remote(
                block, held.at[c, core, rows_of(index), parts[p]], in_send.at[c, p], in_recv.at[c, p],
                section, peer(*relation) * 2 + core,
            ).start()

    def send_feed(c):
        for p, cols in enumerate(parts):
            block = feed.at[rows_of(c), cols]
            spread(block, c, chip, p)
            pltpu.make_async_copy(block, held.at[c, core, rows_of(chip), cols], hop_recv.at[c, p]).start()

    def forward(c):
        for p, cols in enumerate(parts):
            block = held.at[c, core, rows_of(facing), cols]
            wait_for(block, hop_recv.at[c, p])
            spread(block, c, facing, p)

    rows_here = per_core * BLOCK

    @pl.when(section == last)
    def _():
        mine = feed.at[pl.ds(pl.multiple_of(core * rows_here, BLOCK), rows_here)]
        swap = remote(top_hbm.at[:, cols_of(other)], mine, feed_send, feed_recv, section, sibling)
        swap.start()
        keep = pltpu.make_async_copy(top_hbm.at[:, cols_of(core)], mine, own_sem)
        keep.start()
        keep.wait()
        swap.wait()
        for c in range(min(AHEAD, chunks)):
            send_feed(c)

    loads[0].wait()

    def finish(c):
        for p, cols in enumerate(parts):
            wait_for(terms.at[c, pl.ds(0, chips - 1), :, cols], term_recv.at[c, p])
            total = held[c, core, rows_of(chip), cols].astype(F32)
            for j in range(chips):
                total = total + terms[c, j, :, cols].astype(F32)
            result[c, :, cols] = total.astype(BF16)

            @pl.when(section > 0)
            def _():
                remote(
                    result.at[c, :, cols], held.at[c, core, rows_of(chip), cols],
                    hop_send.at[c, p], hop_recv.at[c, p], section - 1, facing * 2 + core,
                ).start()

        place = lax.rem(c, per_core)

        @pl.when(lax.div(c, per_core) == core)
        def _():
            out[core, rows_of(place), :] = result[c]

        @pl.when(lax.div(c, per_core) == other)
        def _():
            remote(
                result.at[c], out.at[core, rows_of(place)], out_send, out_recv, section, sibling
            ).start()

    def chunk_step(c, carry):
        act[...] = gelu(gate[:, c].reshape(chips * BLOCK, -1).astype(F32))

        for p, cols in enumerate(parts):
            @pl.when(section == last)
            def _():
                wait_for(held.at[c, core, rows_of(chip), cols], hop_recv.at[c, p])

            wait_for(terms.at[c, pl.ds(0, chips - 1), :, cols], in_recv.at[c, p])
            remote(
                held.at[c, core, :, cols], held.at[c, core, :, cols], swap_send.at[c, p], swap_recv.at[c, p],
                section, sibling,
            ).start()
            term = lax.dot_general(
                held[c, core, :, cols], down[core, cols, :], NN, preferred_element_type=F32
            )
            hidden[...] = term if p == 0 else hidden[...] + term

        @pl.when((section < last) & (c + 1 < chunks))
        def _():
            forward(c + 1)

        total = hidden[...]
        for p, cols in enumerate(parts):
            wait_for(held.at[c, other, :, cols], swap_recv.at[c, p])
            total = total + lax.dot_general(
                held[c, other, :, cols], down[other, cols, :], NN, preferred_element_type=F32
            )
        grad_up[...] = (total * act[...]).astype(BF16)

        for p, cols in enumerate(parts):
            sib_part[c, :, cols] = lax.dot_general(
                grad_up[...], up[other, :, cols], NN, preferred_element_type=F32
            ).astype(BF16)
            remote(
                sib_part.at[c, :, cols], sib_recv.at[c, :, cols], part_send.at[c, p], part_recv.at[c, p],
                section, sibling,
            ).start()
        own_part[...] = lax.dot_general(grad_up[...], up[core], NN, preferred_element_type=F32)

        @pl.when(c > 0)
        def _():
            finish(c - 1)

        for p, cols in enumerate(parts):
            wait_for(sib_recv.at[c, :, cols], part_recv.at[c, p])
            pair[c, :, cols] = (own_part[:, cols] + sib_recv[c, :, cols].astype(F32)).astype(BF16)
            for relation in ORDER:
                to_chip = peer(*relation)
                remote(
                    pair.at[c, rows_of(to_chip), cols], terms.at[c, chip, :, cols],
                    term_send.at[c, p], term_recv.at[c, p], section, to_chip * 2 + core,
                ).start()
        terms[c, chip] = pair[c, rows_of(chip), :]

        @pl.when((section == last) & (c + AHEAD < chunks))
        def _():
            send_feed(c + AHEAD)

        return carry

    tiles = half // 128

    def turn_down(i, carry):
        for h in range(2):
            down[h, pl.ds(pl.multiple_of(i * 128, 128), 128), :] = down_raw[
                :, pl.ds(pl.multiple_of(h * half + i * 128, 128), 128)
            ].T
        return carry

    def turn_up(i, carry):
        for h in range(2):
            up[h, :, pl.ds(pl.multiple_of(i * 128, 128), 128)] = up_raw[
                pl.ds(pl.multiple_of(h * half + i * 128, 128), 128), :
            ].T
        return carry

    loads[1].wait()
    lax.fori_loop(0, tiles, turn_down, 0)
    loads[2].wait()
    lax.fori_loop(0, tiles, turn_up, 0)

    @pl.when(section < last)
    def _():
        forward(0)

    lax.fori_loop(0, chunks, chunk_step, 0)
    finish(chunks - 1)

    wait_for(out.at[other], out_recv)
    stores = [
        pltpu.make_async_copy(out.at[h], out_hbm.at[:, pl.ds(h * half, half)], store_sem.at[h])
        for h in range(2)
    ]
    for store in stores:
        store.start()

    def drain(c, carry):
        for p, cols in enumerate(parts):
            seven = terms.at[c, pl.ds(0, chips - 1), :, cols]
            wait_for(held.at[c, core, :, cols], swap_send.at[c, p])
            wait_for(sib_part.at[c, :, cols], part_send.at[c, p])
            wait_for(seven, term_send.at[c, p])
            wait_for(seven, in_send.at[c, p])

            @pl.when(section > 0)
            def _():
                wait_for(result.at[c, :, cols], hop_send.at[c, p])

        return carry

    lax.fori_loop(0, chunks, drain, 0)
    wait_for(out.at[core], out_send)
    for store in stores:
        store.wait()


def on_device(sections, top_grad, down_weight, up_weight, gate_pre):
    row_count, features = top_grad.shape[-2:]
    units = gate_pre.shape[-1]
    tokens = gate_pre.shape[2]
    devices = lax.axis_size("tensor")
    chips = devices // 2
    chunks = 2 * row_count // BLOCK
    half = features // 2
    rows = chips * BLOCK
    gate = gate_pre.reshape(chips, chunks, BLOCK, units)
    dma = pltpu.SemaphoreType.DMA
    produced = pl.pallas_call(
        functools.partial(kernel, sections, chips, chunks),
        name="chain",
        out_shape=jax.ShapeDtypeStruct((row_count, features), BF16),
        in_specs=[pl.BlockSpec(memory_space=pl.ANY)] * 4,
        out_specs=pl.BlockSpec(memory_space=pl.ANY),
        scratch_shapes=[
            pltpu.VMEM((units, features), BF16),
            pltpu.VMEM((features, units), BF16),
            pltpu.VMEM((2, half, units), BF16),
            pltpu.VMEM((2, units, half), BF16),
            pltpu.VMEM((chips, chunks, BLOCK, units), BF16),
            pltpu.VMEM((2 * row_count, half), BF16),
            pltpu.VMEM((chunks, 2, rows, half), BF16),
            pltpu.VMEM((rows, units), F32),
            pltpu.VMEM((rows, units), F32),
            pltpu.VMEM((rows, units), BF16),
            pltpu.VMEM((rows, half), F32),
            pltpu.VMEM((chunks, rows, half), BF16),
            pltpu.VMEM((chunks, rows, half), BF16),
            pltpu.VMEM((chunks, rows, half), BF16),
            pltpu.VMEM((chunks, chips, BLOCK, half), BF16),
            pltpu.VMEM((chunks, BLOCK, half), BF16),
            pltpu.VMEM((2, row_count, half), BF16),
            dma((3,)),
            dma,
            dma,
            dma,
            dma((chunks, 2)),
            dma((chunks, 2)),
            dma((chunks, 2)),
            dma((chunks, 2)),
            dma((chunks, 2)),
            dma((chunks, 2)),
            dma((chunks, 2)),
            dma((chunks, 2)),
            dma((chunks, 2)),
            dma((chunks, 2)),
            dma,
            dma,
            dma((2,)),
        ],
        compiler_params=pltpu.CompilerParams(
            collective_id=0, has_side_effects=True, vmem_limit_bytes=60 * 1024 * 1024
        ),
    )(top_grad[0], down_weight[0], up_weight[0], gate)
    return produced[None, None]


def solution(mesh):
    placed = (
        P(None, "tensor", None),
        P("section", "tensor", None),
        P("section", None, "tensor"),
        P("section", None, None, "tensor"),
    )
    return jax.shard_map(
        functools.partial(on_device, mesh.shape["section"]),
        mesh=mesh,
        in_specs=placed,
        out_specs=P("section", None, "tensor", None),
        check_vma=False,
    )
```

```python
import functools

import jax
import jax.numpy as jnp
from jax import lax
from jax.experimental import pallas as pl
from jax.experimental.pallas import tpu as pltpu
from jax.sharding import PartitionSpec as P

MESH = pl.DeviceIdType.MESH
BLOCK = 16
ORDER = ((2, 1), (1, 1), (3, 1), (2, 0), (1, 0), (3, 0), (0, 1))
AHEAD = 3
F32 = jnp.float32
BF16 = jnp.bfloat16
NN = (((1,), (0,)), ((), ()))


def gelu(v):
    return 0.5 * v * (1.0 + jnp.tanh(0.7978845608028654 * (v + 0.044715 * (v * v * v))))


def kernel(
    sections, chips, chunks,
    top_hbm, down_hbm, up_hbm, gate_hbm, out_hbm,
    down_raw, up_raw, down, up, gate, feed, held, act, hidden, grad_up, own_part, sib_part, sib_recv, pair, terms, result,
    load_sem, feed_send, feed_recv, own_sem, hop_send, hop_recv, in_send, in_recv, swap_send, swap_recv, part_send, part_recv,
    term_send, term_recv, out_send, out_recv, out_own,
):
    section = lax.axis_index("section")
    tensor = lax.axis_index("tensor")
    chip = lax.div(tensor, 2)
    core = lax.rem(tensor, 2)
    other = 1 - core
    sibling = chip * 2 + other
    half = held.shape[-1]
    per_core = chunks // 2
    last = sections - 1

    def wait_for(ref, sem):
        pltpu.make_async_copy(ref, ref, sem).wait()

    def remote(src, dst, send, recv, to_section, to_tensor):
        return pltpu.make_async_remote_copy(
            src_ref=src, dst_ref=dst, send_sem=send, recv_sem=recv,
            device_id={"section": to_section, "tensor": to_tensor}, device_id_type=MESH,
        )

    def peer(step, flip):
        return lax.rem(lax.div(chip, 2) + step, chips // 2) * 2 + lax.rem(chip + flip, 2)

    first = half // 256 * 128
    parts = [pl.ds(0, first), pl.ds(first, half - first)]

    def rows_of(index):
        return pl.ds(pl.multiple_of(index * BLOCK, BLOCK), BLOCK)

    def cols_of(index):
        return pl.ds(pl.multiple_of(index * half, 128), half)

    loads = [
        pltpu.make_async_copy(gate_hbm, gate, load_sem.at[0]),
        pltpu.make_async_copy(down_hbm, down_raw, load_sem.at[1]),
        pltpu.make_async_copy(up_hbm, up_raw, load_sem.at[2]),
    ]
    for load in loads:
        load.start()

    barrier = pltpu.get_barrier_semaphore()

    def greet(to_section, to_tensor):
        pl.semaphore_signal(
            barrier, inc=1, device_id={"section": to_section, "tensor": to_tensor}, device_id_type=MESH
        )

    greet(section, sibling)
    for step in range(1, chips):
        greet(section, lax.rem(chip + step, chips) * 2 + core)

    facing = chip + 1 - 2 * lax.rem(chip, 2)

    @pl.when(section > 0)
    def _():
        greet(section - 1, facing * 2 + core)

    @pl.when(section < last)
    def _():
        greet(section + 1, facing * 2 + core)

    pl.semaphore_wait(barrier, chips + jnp.where(section > 0, 1, 0) + jnp.where(section < last, 1, 0))

    def spread(block, c, index, p):
        for relation in ORDER:
            remote(
                block, held.at[c, core, rows_of(index), parts[p]], in_send, in_recv.at[c, p],
                section, peer(*relation) * 2 + core,
            ).start()

    def send_feed(c):
        for p, cols in enumerate(parts):
            block = feed.at[rows_of(c), cols]
            spread(block, c, chip, p)
            pltpu.make_async_copy(block, held.at[c, core, rows_of(chip), cols], hop_recv.at[c, p]).start()

    def forward(c):
        for p, cols in enumerate(parts):
            block = held.at[c, core, rows_of(facing), cols]
            wait_for(block, hop_recv.at[c, p])
            spread(block, c, facing, p)

    rows_here = per_core * BLOCK

    @pl.when(section == last)
    def _():
        mine = feed.at[pl.ds(pl.multiple_of(core * rows_here, BLOCK), rows_here)]
        swap = remote(top_hbm.at[:, cols_of(other)], mine, feed_send, feed_recv, section, sibling)
        swap.start()
        keep = pltpu.make_async_copy(top_hbm.at[:, cols_of(core)], mine, own_sem)
        keep.start()
        keep.wait()
        swap.wait()
        for c in range(min(AHEAD, chunks)):
            send_feed(c)

    loads[0].wait()

    def finish_part(c, p):
        cols = parts[p]
        wait_for(terms.at[c, pl.ds(0, chips - 1), :, cols], term_recv.at[c, p])
        total = held[c, core, rows_of(chip), cols].astype(F32)
        for j in range(chips):
            total = total + terms[c, j, :, cols].astype(F32)
        result[c, :, cols] = total.astype(BF16)

        @pl.when(section > 0)
        def _():
            remote(
                result.at[c, :, cols], held.at[c, core, rows_of(chip), cols],
                hop_send, hop_recv.at[c, p], section - 1, facing * 2 + core,
            ).start()

    def place_result(c):
        rows = rows_of(lax.rem(c, per_core))

        @pl.when(lax.div(c, per_core) == core)
        def _():
            pltpu.make_async_copy(result.at[c], out_hbm.at[rows, cols_of(core)], out_own).start()

        @pl.when(lax.div(c, per_core) == other)
        def _():
            remote(
                result.at[c], out_hbm.at[rows, cols_of(core)], out_send, out_recv, section, sibling
            ).start()

    def chunk_step(c, carry):
        act[...] = gelu(gate[:, c].reshape(chips * BLOCK, -1).astype(F32))

        for p, cols in enumerate(parts):
            @pl.when(section == last)
            def _():
                wait_for(held.at[c, core, rows_of(chip), cols], hop_recv.at[c, p])

            wait_for(terms.at[c, pl.ds(0, chips - 1), :, cols], in_recv.at[c, p])
            remote(
                held.at[c, core, :, cols], held.at[c, core, :, cols], swap_send, swap_recv.at[c, p],
                section, sibling,
            ).start()
            term = lax.dot_general(
                held[c, core, :, cols], down[core, cols, :], NN, preferred_element_type=F32
            )
            hidden[...] = term if p == 0 else hidden[...] + term

        @pl.when((section < last) & (c + 1 < chunks))
        def _():
            forward(c + 1)

        total = hidden[...]
        for p, cols in enumerate(parts):
            wait_for(held.at[c, other, :, cols], swap_recv.at[c, p])
            total = total + lax.dot_general(
                held[c, other, :, cols], down[other, cols, :], NN, preferred_element_type=F32
            )
        grad_up[...] = (total * act[...]).astype(BF16)

        for p, cols in enumerate(parts):
            sib_part[c, :, cols] = lax.dot_general(
                grad_up[...], up[other, :, cols], NN, preferred_element_type=F32
            ).astype(BF16)
            remote(
                sib_part.at[c, :, cols], sib_recv.at[c, :, cols], part_send, part_recv.at[c, p],
                section, sibling,
            ).start()

        @pl.when(c > 0)
        def _():
            finish_part(c - 1, 0)

        own_part[...] = lax.dot_general(grad_up[...], up[core], NN, preferred_element_type=F32)

        for p, cols in enumerate(parts):
            wait_for(sib_recv.at[c, :, cols], part_recv.at[c, p])
            pair[c, :, cols] = (own_part[:, cols] + sib_recv[c, :, cols].astype(F32)).astype(BF16)
            for relation in ORDER:
                to_chip = peer(*relation)
                remote(
                    pair.at[c, rows_of(to_chip), cols], terms.at[c, chip, :, cols],
                    term_send, term_recv.at[c, p], section, to_chip * 2 + core,
                ).start()

            if p == 0:
                @pl.when(c > 0)
                def _():
                    finish_part(c - 1, 1)
                    place_result(c - 1)

        terms[c, chip] = pair[c, rows_of(chip), :]

        @pl.when((section == last) & (c + AHEAD < chunks))
        def _():
            send_feed(c + AHEAD)

        return carry

    tiles = half // 128

    def turn_down(i, carry):
        for h in range(2):
            down[h, pl.ds(pl.multiple_of(i * 128, 128), 128), :] = down_raw[
                :, pl.ds(pl.multiple_of(h * half + i * 128, 128), 128)
            ].T
        return carry

    def turn_up(i, carry):
        for h in range(2):
            up[h, :, pl.ds(pl.multiple_of(i * 128, 128), 128)] = up_raw[
                pl.ds(pl.multiple_of(h * half + i * 128, 128), 128), :
            ].T
        return carry

    loads[1].wait()
    lax.fori_loop(0, tiles, turn_down, 0)
    loads[2].wait()
    lax.fori_loop(0, tiles, turn_up, 0)

    @pl.when(section < last)
    def _():
        forward(0)

    lax.fori_loop(0, chunks, chunk_step, 0)
    for p in range(len(parts)):
        finish_part(chunks - 1, p)
    place_result(chunks - 1)

    wait_for(feed.at[pl.ds(0, rows_here)], out_own)
    wait_for(feed.at[pl.ds(0, rows_here)], out_recv)
    wait_for(held.at[:, core], swap_send)
    wait_for(sib_part, part_send)
    wait_for(terms.at[:, pl.ds(0, chips - 1)], term_send)
    wait_for(terms.at[:, pl.ds(0, chips - 1)], in_send)

    @pl.when(section > 0)
    def _():
        wait_for(result, hop_send)

    wait_for(feed.at[pl.ds(0, rows_here)], out_send)


def on_device(sections, top_grad, down_weight, up_weight, gate_pre):
    row_count, features = top_grad.shape[-2:]
    units = gate_pre.shape[-1]
    tokens = gate_pre.shape[2]
    devices = lax.axis_size("tensor")
    chips = devices // 2
    chunks = 2 * row_count // BLOCK
    half = features // 2
    rows = chips * BLOCK
    gate = gate_pre.reshape(chips, chunks, BLOCK, units)
    dma = pltpu.SemaphoreType.DMA
    produced = pl.pallas_call(
        functools.partial(kernel, sections, chips, chunks),
        name="chain",
        out_shape=jax.ShapeDtypeStruct((row_count, features), BF16),
        in_specs=[pl.BlockSpec(memory_space=pl.ANY)] * 4,
        out_specs=pl.BlockSpec(memory_space=pl.ANY),
        scratch_shapes=[
            pltpu.VMEM((units, features), BF16),
            pltpu.VMEM((features, units), BF16),
            pltpu.VMEM((2, half, units), BF16),
            pltpu.VMEM((2, units, half), BF16),
            pltpu.VMEM((chips, chunks, BLOCK, units), BF16),
            pltpu.VMEM((2 * row_count, half), BF16),
            pltpu.VMEM((chunks, 2, rows, half), BF16),
            pltpu.VMEM((rows, units), F32),
            pltpu.VMEM((rows, units), F32),
            pltpu.VMEM((rows, units), BF16),
            pltpu.VMEM((rows, half), F32),
            pltpu.VMEM((chunks, rows, half), BF16),
            pltpu.VMEM((chunks, rows, half), BF16),
            pltpu.VMEM((chunks, rows, half), BF16),
            pltpu.VMEM((chunks, chips, BLOCK, half), BF16),
            pltpu.VMEM((chunks, BLOCK, half), BF16),
            dma((3,)),
            dma,
            dma,
            dma,
            dma,
            dma((chunks, 2)),
            dma,
            dma((chunks, 2)),
            dma,
            dma((chunks, 2)),
            dma,
            dma((chunks, 2)),
            dma,
            dma((chunks, 2)),
            dma,
            dma,
            dma,
        ],
        compiler_params=pltpu.CompilerParams(
            collective_id=0, has_side_effects=True, vmem_limit_bytes=60 * 1024 * 1024
        ),
    )(top_grad[0], down_weight[0], up_weight[0], gate)
    return produced[None, None]


def solution(mesh):
    placed = (
        P(None, "tensor", None),
        P("section", "tensor", None),
        P("section", None, "tensor"),
        P("section", None, None, "tensor"),
    )
    return jax.shard_map(
        functools.partial(on_device, mesh.shape["section"]),
        mesh=mesh,
        in_specs=placed,
        out_specs=P("section", None, "tensor", None),
        check_vma=False,
    )
```

```python
import functools

import jax
import jax.numpy as jnp
from jax import lax
from jax.experimental import pallas as pl
from jax.experimental.pallas import tpu as pltpu
from jax.sharding import PartitionSpec as P

MESH = pl.DeviceIdType.MESH
BLOCK = 16
ORDER = ((2, 1), (1, 1), (3, 1), (0, 1), (2, 0), (1, 0), (3, 0))
AHEAD = 3
F32 = jnp.float32
BF16 = jnp.bfloat16
NN = (((1,), (0,)), ((), ()))


def gelu(v):
    return 0.5 * v * (1.0 + jnp.tanh(0.7978845608028654 * (v + 0.044715 * (v * v * v))))


def kernel(
    sections, chips, chunks,
    top_hbm, down_hbm, up_hbm, gate_hbm, out_hbm,
    down_raw, up_raw, down, up, gate, feed, held, act, hidden, grad_up, own_part, sib_part, sib_recv, pair, terms, result,
    load_sem, feed_send, feed_recv, own_sem, hop_send, hop_recv, in_send, in_recv, swap_send, swap_recv, part_send, part_recv,
    term_send, term_recv, out_send, out_recv, out_own,
):
    section = lax.axis_index("section")
    tensor = lax.axis_index("tensor")
    chip = lax.div(tensor, 2)
    core = lax.rem(tensor, 2)
    other = 1 - core
    sibling = chip * 2 + other
    half = held.shape[-1]
    per_core = chunks // 2
    last = sections - 1

    def wait_for(ref, sem):
        pltpu.make_async_copy(ref, ref, sem).wait()

    def remote(src, dst, send, recv, to_section, to_tensor):
        return pltpu.make_async_remote_copy(
            src_ref=src, dst_ref=dst, send_sem=send, recv_sem=recv,
            device_id={"section": to_section, "tensor": to_tensor}, device_id_type=MESH,
        )

    def peer(step, flip):
        return lax.rem(lax.div(chip, 2) + step, chips // 2) * 2 + lax.rem(chip + flip, 2)

    first = half // 256 * 128
    parts = [pl.ds(0, first), pl.ds(first, half - first)]

    def rows_of(index):
        return pl.ds(pl.multiple_of(index * BLOCK, BLOCK), BLOCK)

    def cols_of(index):
        return pl.ds(pl.multiple_of(index * half, 128), half)

    loads = [
        pltpu.make_async_copy(gate_hbm, gate, load_sem.at[0]),
        pltpu.make_async_copy(down_hbm, down_raw, load_sem.at[1]),
        pltpu.make_async_copy(up_hbm, up_raw, load_sem.at[2]),
    ]
    for load in loads:
        load.start()

    barrier = pltpu.get_barrier_semaphore()

    def greet(to_section, to_tensor):
        pl.semaphore_signal(
            barrier, inc=1, device_id={"section": to_section, "tensor": to_tensor}, device_id_type=MESH
        )

    greet(section, sibling)
    for step in range(1, chips):
        greet(section, lax.rem(chip + step, chips) * 2 + core)

    facing = chip + 1 - 2 * lax.rem(chip, 2)

    @pl.when(section > 0)
    def _():
        greet(section - 1, facing * 2 + core)

    @pl.when(section < last)
    def _():
        greet(section + 1, facing * 2 + core)

    pl.semaphore_wait(barrier, chips + jnp.where(section > 0, 1, 0) + jnp.where(section < last, 1, 0))

    def spread(block, c, index, p):
        for relation in ORDER:
            remote(
                block, held.at[c, core, rows_of(index), parts[p]], in_send, in_recv.at[c, p],
                section, peer(*relation) * 2 + core,
            ).start()

    def send_feed(c):
        for p, cols in enumerate(parts):
            block = feed.at[rows_of(c), cols]
            spread(block, c, chip, p)
            pltpu.make_async_copy(block, held.at[c, core, rows_of(chip), cols], hop_recv.at[c, p]).start()

    def forward(c):
        for p, cols in enumerate(parts):
            block = held.at[c, core, rows_of(facing), cols]
            wait_for(block, hop_recv.at[c, p])
            spread(block, c, facing, p)

    rows_here = per_core * BLOCK

    @pl.when(section == last)
    def _():
        ready = min(AHEAD, per_core)
        pieces = [(0, ready * BLOCK), (ready * BLOCK, rows_here - ready * BLOCK)]
        moves = []
        for q, (start, size) in enumerate(pieces):
            if size:
                mine = feed.at[pl.ds(pl.multiple_of(core * rows_here + start, BLOCK), size)]
                theirs = top_hbm.at[pl.ds(start, size), cols_of(other)]
                swap = remote(theirs, mine, feed_send.at[q], feed_recv.at[q], section, sibling)
                keep = pltpu.make_async_copy(top_hbm.at[pl.ds(start, size), cols_of(core)], mine, own_sem.at[q])
                swap.start()
                keep.start()
                moves.append((swap, keep))
        for c in range(min(AHEAD, chunks)):
            if c % ready == 0 and c // ready < len(moves):
                for move in moves[c // ready]:
                    move.wait()
            send_feed(c)
        for swap, keep in moves[(min(AHEAD, chunks) - 1) // ready + 1:]:
            swap.wait()
            keep.wait()

    loads[0].wait()

    def finish_part(c, p):
        cols = parts[p]
        wait_for(terms.at[c, pl.ds(0, chips - 1), :, cols], term_recv.at[c, p])
        total = held[c, core, rows_of(chip), cols].astype(F32)
        for j in range(chips):
            total = total + terms[c, j, :, cols].astype(F32)
        result[c, :, cols] = total.astype(BF16)

        @pl.when(section > 0)
        def _():
            remote(
                result.at[c, :, cols], held.at[c, core, rows_of(chip), cols],
                hop_send, hop_recv.at[c, p], section - 1, facing * 2 + core,
            ).start()

    def place_result(c):
        rows = rows_of(lax.rem(c, per_core))

        @pl.when(lax.div(c, per_core) == core)
        def _():
            pltpu.make_async_copy(result.at[c], out_hbm.at[rows, cols_of(core)], out_own).start()

        @pl.when(lax.div(c, per_core) == other)
        def _():
            remote(
                result.at[c], out_hbm.at[rows, cols_of(core)], out_send, out_recv, section, sibling
            ).start()

    def chunk_step(c, carry):
        act[...] = gelu(gate[:, c].reshape(chips * BLOCK, -1).astype(F32))

        for p, cols in enumerate(parts):
            @pl.when(section == last)
            def _():
                wait_for(held.at[c, core, rows_of(chip), cols], hop_recv.at[c, p])

            wait_for(terms.at[c, pl.ds(0, chips - 1), :, cols], in_recv.at[c, p])
            remote(
                held.at[c, core, :, cols], held.at[c, core, :, cols], swap_send, swap_recv.at[c, p],
                section, sibling,
            ).start()
            term = lax.dot_general(
                held[c, core, :, cols], down[core, cols, :], NN, preferred_element_type=F32
            )
            hidden[...] = term if p == 0 else hidden[...] + term

        @pl.when((section < last) & (c + 1 < chunks))
        def _():
            forward(c + 1)

        total = hidden[...]
        for p, cols in enumerate(parts):
            wait_for(held.at[c, other, :, cols], swap_recv.at[c, p])
            total = total + lax.dot_general(
                held[c, other, :, cols], down[other, cols, :], NN, preferred_element_type=F32
            )
        grad_up[...] = (total * act[...]).astype(BF16)

        for p, cols in enumerate(parts):
            sib_part[c, :, cols] = lax.dot_general(
                grad_up[...], up[other, :, cols], NN, preferred_element_type=F32
            ).astype(BF16)
            remote(
                sib_part.at[c, :, cols], sib_recv.at[c, :, cols], part_send, part_recv.at[c, p],
                section, sibling,
            ).start()

        @pl.when(c > 0)
        def _():
            finish_part(c - 1, 0)

        own_part[...] = lax.dot_general(grad_up[...], up[core], NN, preferred_element_type=F32)

        for p, cols in enumerate(parts):
            wait_for(sib_recv.at[c, :, cols], part_recv.at[c, p])
            pair[c, :, cols] = (own_part[:, cols] + sib_recv[c, :, cols].astype(F32)).astype(BF16)
            for relation in ORDER:
                to_chip = peer(*relation)
                remote(
                    pair.at[c, rows_of(to_chip), cols], terms.at[c, chip, :, cols],
                    term_send, term_recv.at[c, p], section, to_chip * 2 + core,
                ).start()

            if p == 0:
                @pl.when(c > 0)
                def _():
                    finish_part(c - 1, 1)
                    place_result(c - 1)

        terms[c, chip] = pair[c, rows_of(chip), :]

        @pl.when((section == last) & (c + AHEAD < chunks))
        def _():
            send_feed(c + AHEAD)

        return carry

    tiles = half // 128

    def turn_down(i, carry):
        for h in range(2):
            down[h, pl.ds(pl.multiple_of(i * 128, 128), 128), :] = down_raw[
                :, pl.ds(pl.multiple_of(h * half + i * 128, 128), 128)
            ].T
        return carry

    def turn_up(i, carry):
        for h in range(2):
            up[h, :, pl.ds(pl.multiple_of(i * 128, 128), 128)] = up_raw[
                pl.ds(pl.multiple_of(h * half + i * 128, 128), 128), :
            ].T
        return carry

    loads[1].wait()
    lax.fori_loop(0, tiles, turn_down, 0)
    loads[2].wait()
    lax.fori_loop(0, tiles, turn_up, 0)

    @pl.when(section < last)
    def _():
        forward(0)

    lax.fori_loop(0, chunks, chunk_step, 0)
    for p in range(len(parts)):
        finish_part(chunks - 1, p)
    place_result(chunks - 1)

    wait_for(feed.at[pl.ds(0, rows_here)], out_own)
    wait_for(feed.at[pl.ds(0, rows_here)], out_recv)
    wait_for(held.at[:, core], swap_send)
    wait_for(sib_part, part_send)
    wait_for(terms.at[:, pl.ds(0, chips - 1)], term_send)
    wait_for(terms.at[:, pl.ds(0, chips - 1)], in_send)

    @pl.when(section > 0)
    def _():
        wait_for(result, hop_send)

    wait_for(feed.at[pl.ds(0, rows_here)], out_send)


def on_device(sections, top_grad, down_weight, up_weight, gate_pre):
    row_count, features = top_grad.shape[-2:]
    units = gate_pre.shape[-1]
    tokens = gate_pre.shape[2]
    devices = lax.axis_size("tensor")
    chips = devices // 2
    chunks = 2 * row_count // BLOCK
    half = features // 2
    rows = chips * BLOCK
    gate = gate_pre.reshape(chips, chunks, BLOCK, units)
    dma = pltpu.SemaphoreType.DMA
    produced = pl.pallas_call(
        functools.partial(kernel, sections, chips, chunks),
        name="chain",
        out_shape=jax.ShapeDtypeStruct((row_count, features), BF16),
        in_specs=[pl.BlockSpec(memory_space=pl.ANY)] * 4,
        out_specs=pl.BlockSpec(memory_space=pl.ANY),
        scratch_shapes=[
            pltpu.VMEM((units, features), BF16),
            pltpu.VMEM((features, units), BF16),
            pltpu.VMEM((2, half, units), BF16),
            pltpu.VMEM((2, units, half), BF16),
            pltpu.VMEM((chips, chunks, BLOCK, units), BF16),
            pltpu.VMEM((2 * row_count, half), BF16),
            pltpu.VMEM((chunks, 2, rows, half), BF16),
            pltpu.VMEM((rows, units), F32),
            pltpu.VMEM((rows, units), F32),
            pltpu.VMEM((rows, units), BF16),
            pltpu.VMEM((rows, half), F32),
            pltpu.VMEM((chunks, rows, half), BF16),
            pltpu.VMEM((chunks, rows, half), BF16),
            pltpu.VMEM((chunks, rows, half), BF16),
            pltpu.VMEM((chunks, chips, BLOCK, half), BF16),
            pltpu.VMEM((chunks, BLOCK, half), BF16),
            dma((3,)),
            dma((2,)),
            dma((2,)),
            dma((2,)),
            dma,
            dma((chunks, 2)),
            dma,
            dma((chunks, 2)),
            dma,
            dma((chunks, 2)),
            dma,
            dma((chunks, 2)),
            dma,
            dma((chunks, 2)),
            dma,
            dma,
            dma,
        ],
        compiler_params=pltpu.CompilerParams(
            collective_id=0, has_side_effects=True, vmem_limit_bytes=60 * 1024 * 1024
        ),
    )(top_grad[0], down_weight[0], up_weight[0], gate)
    return produced[None, None]


def solution(mesh):
    placed = (
        P(None, "tensor", None),
        P("section", "tensor", None),
        P("section", None, "tensor"),
        P("section", None, None, "tensor"),
    )
    return jax.shard_map(
        functools.partial(on_device, mesh.shape["section"]),
        mesh=mesh,
        in_specs=placed,
        out_specs=P("section", None, "tensor", None),
        check_vma=False,
    )
```
